32 devices in a mesh: fsdp: 4 (over y, x), tensor: 8 (over z, core).
Axes of the slice: x: 2, y: 2, z: 4, core: 2. Of those that a mesh axis runs over, the one named last changes fastest.
Arguments:
- tokens: bfloat16 [640, 4096], P('fsdp', 'tensor'), may hold values from -6 to 6
- out_grad: bfloat16 [640, 4096], P('fsdp', 'tensor'), may hold values from -0.26953125 to 0.26953125
- gate_weight: bfloat16 [4096, 16384], P('fsdp', 'tensor'), may hold values from -0.125 to 0.125
- up_weight: bfloat16 [4096, 16384], P('fsdp', 'tensor'), may hold values from -0.125 to 0.125
- down_weight: bfloat16 [16384, 4096], P('tensor', 'fsdp'), may hold values from -1.796875 to 1.796875
- gate_mask: int32 [32, 128], replicated, may hold values from 0 to 1, as said below
- up_mask: int32 [32, 128], replicated, may hold values from 0 to 1, as said below
- down_mask: int32 [128, 32], replicated, may hold values from 0 to 1, as said below
Outputs:
- input_grad: bfloat16 [640, 4096], P('fsdp', 'tensor')
- down_grad: bfloat16 [16384, 4096], P('tensor', 'fsdp')
The draws below stay inside these ranges and needn't reach their ends.
Inputs may be any that keep to these rules, and one draw needn't show every extreme that they name: `gate_mask`: seen as regions of 8 x 16 blocks (the block rows of one index of fsdp and the block columns of one index of tensor), each region keeps between 32 and 80 blocks, and some region keeps exactly 80. `up_mask`: seen as regions of 8 x 16 blocks as for gate_mask, each region keeps between 32 and 80 blocks, and some region keeps exactly 80. `down_mask`: seen as regions of 16 x 8 blocks (the block rows of one index of tensor and the block columns of one index of fsdp), each region keeps between 32 and 80 blocks, and some region keeps exactly 80.
All inputs are finite; a program needn't handle non-finite values.
Results may differ from the reference program's by a relative error of at most 0.013.
Values may be sent and summed in bfloat16 or wider, within the bound.
No kernel may reach another device: no remote copies, remote signals or barrier semaphores. Data moves between devices by JAX's collectives and lax.ppermute only.
A program may use at most 256 MiB of HBM per device.

```python
import jax
import jax.numpy as jnp
from jax import lax

D = 4096
FF = 16384
BLOCK = 128
TOK_DEV = 160
TOKENS = 640
DB = 32
FB = 128
RB = 8
CB = 16
N_FSDP = 4
N_TENSOR = 8


def region_flags(key, row_regions, col_regions, rows_each, cols_each):
    region_size = rows_each * cols_each
    fewest = region_size // 4
    largest = region_size * 5 // 8
    count_key, pick_key, order_key = jax.random.split(key, 3)
    regions = row_regions * col_regions
    counts = jax.random.randint(count_key, (regions,), fewest, largest + 1)
    picked = jax.random.randint(pick_key, (), 0, regions)
    counts = jnp.where(jnp.arange(regions) == picked, largest, counts)
    orders = jax.vmap(lambda subkey: jax.random.permutation(subkey, region_size))(jax.random.split(order_key, regions))
    kept_flags = (orders < counts[:, None]).astype(jnp.int32)
    kept_flags = kept_flags.reshape(row_regions, col_regions, rows_each, cols_each).transpose(0, 2, 1, 3)
    return kept_flags.reshape(row_regions * rows_each, col_regions * cols_each)


def draw_gate_mask(key, part):
    key = jax.random.fold_in(key, 11)
    return region_flags(key, DB // RB, FB // CB, RB, CB)


def draw_up_mask(key, part):
    key = jax.random.fold_in(key, 12)
    return region_flags(key, DB // RB, FB // CB, RB, CB)


def draw_down_mask(key, part):
    key = jax.random.fold_in(key, 13)
    return region_flags(key, FB // CB, DB // RB, CB, RB)


def steps_of(own_key, extent, shards, least, high):
    level = 1.0
    for position, parts in shards:
        steps = jax.random.uniform(jax.random.fold_in(jax.random.fold_in(own_key, 6), position), (parts,), jnp.float32, least / len(shards), high / len(shards))
        level = level * jnp.repeat(jnp.exp(steps), extent[position] // parts).reshape((-1,) + (1,) * (len(extent) - 1 - position))
    return level


def noise(rng, extent, width, limit, cuts=(), dtype=jnp.bfloat16):
    result = width * jax.random.normal(rng, extent, jnp.float32)
    if cuts:
        result = result * steps_of(rng, extent, cuts, -0.22, 0.18)
    return jnp.clip(result, -limit, limit).astype(dtype)


def setup_inputs(seed: int = 0) -> dict:
    keys = jax.random.split(jax.random.key(seed), 9)
    tokens = noise(keys[0], (TOKENS, D), 1.0, 6.0, ((0, 4), (1, 8)))
    out_grad = noise(keys[1], (TOKENS, D), 0.045, 0.26953125, ((0, 4), (1, 8)))
    gate_weight = noise(keys[2], (D, FF), (D // 2) ** -0.5, 0.125, ((0, 4), (1, 8)))
    up_weight = noise(keys[3], (D, FF), (D // 2) ** -0.5, 0.125, ((0, 4), (1, 8)))
    down_weight = noise(keys[4], (FF, D), 0.3, 1.796875, ((0, 8), (1, 4)))
    gate_mask = draw_gate_mask(jax.random.fold_in(keys[8], 71), 0)
    up_mask = draw_up_mask(jax.random.fold_in(keys[8], 71), 0)
    down_mask = draw_down_mask(jax.random.fold_in(keys[8], 71), 0)
    return {"tokens": tokens, "out_grad": out_grad, "gate_weight": gate_weight, "up_weight": up_weight, "down_weight": down_weight, "gate_mask": gate_mask, "up_mask": up_mask, "down_mask": down_mask}


def widen_mask(mask_blocks):
    return jnp.repeat(jnp.repeat(mask_blocks, BLOCK, axis=0), BLOCK, axis=1)


def reference(tokens, out_grad, gate_weight, up_weight, down_weight, gate_mask, up_mask, down_mask):
    zero_value = jnp.zeros((), jnp.bfloat16)
    kept_gate = jnp.where(widen_mask(gate_mask) == 1, gate_weight, zero_value)
    kept_up = jnp.where(widen_mask(up_mask) == 1, up_weight, zero_value)
    kept_down = jnp.where(widen_mask(down_mask) == 1, down_weight, zero_value)
    gate_pre = jnp.dot(tokens, kept_gate, preferred_element_type=jnp.float32)
    up_pre = jnp.dot(tokens, kept_up, preferred_element_type=jnp.float32)
    gate_sig = jax.nn.sigmoid(gate_pre)
    gate_act = gate_pre * gate_sig
    hidden = (gate_act * up_pre).astype(jnp.bfloat16)
    hidden_grad = jnp.dot(out_grad, kept_down.T, preferred_element_type=jnp.float32)
    gate_grad = (hidden_grad * up_pre * (gate_sig * (1.0 + gate_pre * (1.0 - gate_sig)))).astype(jnp.bfloat16)
    up_grad = (hidden_grad * gate_act).astype(jnp.bfloat16)
    shard_width = FF // N_TENSOR
    input_sum = jnp.zeros((TOKENS, D), jnp.float32)
    for tensor_index in range(N_TENSOR):
        col_span = slice(tensor_index * shard_width, (tensor_index + 1) * shard_width)
        partial_value = jnp.dot(gate_grad[:, col_span], kept_gate[:, col_span].T, preferred_element_type=jnp.float32)
        partial_value = partial_value + jnp.dot(up_grad[:, col_span], kept_up[:, col_span].T, preferred_element_type=jnp.float32)
        rounded = lax.optimization_barrier(partial_value.astype(jnp.bfloat16))
        input_sum = input_sum + rounded.astype(jnp.float32)
    input_grad = input_sum.astype(jnp.bfloat16)
    weight_sum = jnp.zeros((FF, D), jnp.float32)
    for group_index in range(N_FSDP):
        row_span = slice(group_index * TOK_DEV, (group_index + 1) * TOK_DEV)
        partial_value = jnp.dot(hidden[row_span].T, out_grad[row_span], preferred_element_type=jnp.float32)
        rounded = lax.optimization_barrier(partial_value.astype(jnp.bfloat16))
        weight_sum = weight_sum + rounded.astype(jnp.float32)
    down_grad = jnp.where(widen_mask(down_mask) == 1, weight_sum, jnp.zeros((), jnp.float32)).astype(jnp.bfloat16)
    return input_grad, down_grad
```

```python
import jax
import jax.numpy as jnp
from jax import lax
from jax.sharding import PartitionSpec as P

BLOCK = 128
AXES = ("fsdp", "tensor")


def per_device(
    tokens, out_grad, gate_weight, up_weight, down_weight, gate_mask, up_mask, down_mask
):
    n_f = lax.axis_size("fsdp")
    n_t = lax.axis_size("tensor")
    ratio = n_t // n_f
    rows, width = tokens.shape
    row_blocks = gate_weight.shape[0] // BLOCK
    col_blocks = gate_weight.shape[1] // BLOCK
    f_index = lax.axis_index("fsdp")
    t_index = lax.axis_index("tensor")
    swap = [
        (f * n_t + ratio * a + c, a * n_t + ratio * f + c)
        for f in range(n_f)
        for a in range(n_f)
        for c in range(ratio)
    ]

    def columns_of_owner(x):
        moved = lax.ppermute(x, AXES, swap)
        pieces = lax.all_gather(moved, "tensor", axis=0)
        pieces = pieces.reshape(n_f, ratio, rows, width).transpose(0, 2, 1, 3)
        return pieces.reshape(n_f * rows, ratio * width)

    def keep(weight, mask, row_start, col_start):
        rb, cb = weight.shape[0] // BLOCK, weight.shape[1] // BLOCK
        own = lax.dynamic_slice(mask, (row_start * rb, col_start * cb), (rb, cb))
        wide = jnp.repeat(jnp.repeat(own, BLOCK, axis=0), BLOCK, axis=1)
        return jnp.where(wide == 1, weight, jnp.zeros((), weight.dtype)), wide

    x_cols = columns_of_owner(tokens)
    g_cols = columns_of_owner(out_grad)
    gate, _ = keep(gate_weight, gate_mask, f_index, t_index)
    up, _ = keep(up_weight, up_mask, f_index, t_index)
    down, down_wide = keep(down_weight, down_mask, t_index, f_index)

    def owner_sum(part):
        return lax.psum_scatter(
            part.astype(jnp.bfloat16), "fsdp", scatter_dimension=0, tiled=True
        ).astype(jnp.float32)

    gate_pre = owner_sum(jnp.dot(x_cols, gate, preferred_element_type=jnp.float32))
    up_pre = owner_sum(jnp.dot(x_cols, up, preferred_element_type=jnp.float32))
    hidden_grad = owner_sum(
        lax.dot_general(
            g_cols, down, (((1,), (1,)), ((), ())), preferred_element_type=jnp.float32
        )
    )
    sig = jax.nn.sigmoid(gate_pre)
    act = gate_pre * sig
    hidden = (act * up_pre).astype(jnp.bfloat16)
    gate_grad = (hidden_grad * up_pre * (sig * (1.0 + gate_pre * (1.0 - sig)))).astype(jnp.bfloat16)
    up_grad = (hidden_grad * act).astype(jnp.bfloat16)

    gate_grad = lax.all_gather(gate_grad, "fsdp", axis=0, tiled=True)
    up_grad = lax.all_gather(up_grad, "fsdp", axis=0, tiled=True)
    hidden = lax.all_gather(hidden, "fsdp", axis=0, tiled=True)
    term = lax.dot_general(
        gate_grad, gate, (((1,), (1,)), ((), ())), preferred_element_type=jnp.float32
    ) + lax.dot_general(
        up_grad, up, (((1,), (1,)), ((), ())), preferred_element_type=jnp.float32
    )
    term = term.astype(jnp.bfloat16).reshape(n_f, rows, ratio, width).transpose(0, 2, 1, 3)
    term = term.reshape(n_t, rows, width)
    own_term = lax.psum_scatter(term, "tensor", scatter_dimension=0, tiled=False)
    input_grad = lax.ppermute(own_term, AXES, swap)
    down_grad = lax.dot_general(
        hidden, g_cols, (((0,), (0,)), ((), ())), preferred_element_type=jnp.float32
    )
    down_grad = jnp.where(down_wide == 1, down_grad, 0.0).astype(jnp.bfloat16)
    return (input_grad, down_grad)


def solution(mesh):
    return jax.shard_map(
        per_device,
        mesh=mesh,
        in_specs=(
            P("fsdp", "tensor"),
            P("fsdp", "tensor"),
            P("fsdp", "tensor"),
            P("fsdp", "tensor"),
            P("tensor", "fsdp"),
            P(),
            P(),
            P(),
        ),
        out_specs=(P("fsdp", "tensor"), P("tensor", "fsdp")),
        check_vma=False,
    )
```

```python
import functools

import jax
import jax.numpy as jnp
from jax import lax
from jax.experimental import pallas as pl
from jax.experimental.pallas import tpu as pltpu
from jax.sharding import PartitionSpec as P

BLOCK = 128
AXES = ("fsdp", "tensor")
VMEM_BYTES = 48 * 1024 * 1024


def keep_blocks(weight, flag_of):
    rows = []
    for i in range(weight.shape[0] // BLOCK):
        row = []
        for j in range(weight.shape[1] // BLOCK):
            block = weight[i * BLOCK : (i + 1) * BLOCK, j * BLOCK : (j + 1) * BLOCK]
            row.append(jnp.where(flag_of(i, j) == 1, block, jnp.zeros_like(block)))
        rows.append(jnp.concatenate(row, axis=1))
    return jnp.concatenate(rows, axis=0)


def forward_kernel(order, half, transposed, place, flags, own, other, weight, kept, sent, x_all):
    groups, rows, width = own.shape
    step = pl.program_id(0)
    tile = kept.shape[2]
    blocks = tile // BLOCK

    @pl.when(step == 0)
    def _():
        low = place[1] == 0
        for i in range(groups):
            k = order[i] ^ place[0]
            a, b = own[k], other[k]
            x_all[i * rows : (i + 1) * rows, :width] = jnp.where(low, a, b)
            x_all[i * rows : (i + 1) * rows, width:] = jnp.where(low, b, a)

    first = (half * pl.num_programs(0) + step) * blocks
    if transposed:
        masked = keep_blocks(weight[...], lambda i, j: flags[first + i, j])
        dims = (((1,), (1,)), ((), ()))
    else:
        masked = keep_blocks(weight[...], lambda i, j: flags[i, first + j])
        dims = (((1,), (0,)), ((), ()))
    part = lax.dot_general(x_all[...], masked, dims, preferred_element_type=jnp.float32)
    part = part.reshape(groups, rows, tile)
    kept[...] = part[: groups // 2]
    sent[...] = part[groups // 2 :].astype(jnp.bfloat16)


def forward_half(place, flags, own, other, weight, order, half, transposed):
    groups, rows, width = own.shape
    inner = 2 * width
    span = weight.shape[0 if transposed else 1] // 2
    tile = min(512, span)
    steps = span // tile
    full = pl.BlockSpec((groups, rows, width), lambda j, *_: (0, 0, 0))
    if transposed:
        weight_spec = pl.BlockSpec((tile, inner), lambda j, *_: (half * steps + j, 0))
    else:
        weight_spec = pl.BlockSpec((inner, tile), lambda j, *_: (0, half * steps + j))
    out_spec = pl.BlockSpec((groups // 2, rows, tile), lambda j, *_: (0, 0, j))
    shape = (groups // 2, rows, span)
    return pl.pallas_call(
        functools.partial(forward_kernel, order, half, transposed),
        grid_spec=pltpu.PrefetchScalarGridSpec(
            num_scalar_prefetch=2,
            grid=(steps,),
            in_specs=[full, full, weight_spec],
            out_specs=[out_spec, out_spec],
            scratch_shapes=[pltpu.VMEM((groups * rows, inner), jnp.bfloat16)],
        ),
        out_shape=[
            jax.ShapeDtypeStruct(shape, jnp.float32),
            jax.ShapeDtypeStruct(shape, jnp.bfloat16),
        ],
        compiler_params=pltpu.CompilerParams(vmem_limit_bytes=VMEM_BYTES),
        cost_estimate=pl.CostEstimate(
            flops=2 * groups * rows * inner * span,
            bytes_accessed=2 * inner * (groups * rows + span) + 3 * groups * rows * span,
            transcendentals=0,
        ),
    )(place, flags, own, other, weight)


def input_kernel(groups, own_side, place, gate_flags, up_flags, *refs):
    count = 2 * groups
    pieces, (gate, up, out, stacked) = refs[: 2 * count], refs[2 * count :]
    rows, span = pieces[0].shape
    tile = out.shape[2]
    step = pl.program_id(0)
    tiles = pl.num_programs(0)

    @pl.when(step == 0)
    def _():
        for side in range(2):
            for half in range(2):
                for rel in range(groups):
                    piece = pieces[side * count + half * groups + rel]
                    start = (2 * side + half) * span
                    stacked[rel ^ place[0], :, start : start + span] = piece[...]

    side_of = place[1] if own_side else 1 - place[1]
    first = (side_of * tiles + step) * (tile // BLOCK)
    grads = stacked[...].reshape(groups * rows, 4 * span)
    dims = (((1,), (1,)), ((), ()))
    gate_kept = keep_blocks(gate[...], lambda i, j: gate_flags[first + i, j])
    up_kept = keep_blocks(up[...], lambda i, j: up_flags[first + i, j])
    total = lax.dot_general(
        grads[:, : 2 * span], gate_kept, dims, preferred_element_type=jnp.float32
    ) + lax.dot_general(grads[:, 2 * span :], up_kept, dims, preferred_element_type=jnp.float32)
    out[...] = total.reshape(groups, rows, tile).astype(out.dtype)


def input_side(place, gate_flags, up_flags, pieces, gate, up, groups, width, own_side):
    rows, span = pieces[0].shape
    tile = min(256, width)
    tiles = width // tile
    whole = pl.BlockSpec((rows, span), lambda j, *_: (0, 0))

    def weight_block(j, place, *_):
        side = place[1] if own_side else 1 - place[1]
        return (side * tiles + j, 0)

    weight_spec = pl.BlockSpec((tile, gate.shape[1]), weight_block)
    return pl.pallas_call(
        functools.partial(input_kernel, groups, own_side),
        grid_spec=pltpu.PrefetchScalarGridSpec(
            num_scalar_prefetch=3,
            grid=(tiles,),
            in_specs=[whole] * len(pieces) + [weight_spec, weight_spec],
            out_specs=pl.BlockSpec((groups, rows, tile), lambda j, *_: (0, 0, j)),
            scratch_shapes=[pltpu.VMEM((groups, rows, 4 * span), jnp.bfloat16)],
        ),
        out_shape=jax.ShapeDtypeStruct(
            (groups, rows, width), jnp.float32 if own_side else jnp.bfloat16
        ),
        compiler_params=pltpu.CompilerParams(vmem_limit_bytes=VMEM_BYTES),
        cost_estimate=pl.CostEstimate(
            flops=2 * groups * rows * 4 * span * width,
            bytes_accessed=8 * span * (groups * rows + width) + 4 * groups * rows * width,
            transcendentals=0,
        ),
    )(place, gate_flags, up_flags, *pieces, gate, up)


def down_product(place, flags, own, other, halves):
    groups, rows, width = own.shape
    span = halves[0][0].shape[1]
    tile = min(512, span)
    steps = span // tile
    full = pl.BlockSpec((groups, rows, width), lambda j, *_: (0, 0, 0))

    def kernel(place, flags, *refs):
        first, second = refs[:groups], refs[groups : 2 * groups]
        own, other, out, hidden, grads = refs[2 * groups :]
        step = pl.program_id(0)
        blocks = tile // BLOCK

        @pl.when(step == 0)
        def _():
            low = place[1] == 0
            for rel in range(groups):
                k = rel ^ place[0]
                a, b = own[k], other[k]
                grads[rel * rows : (rel + 1) * rows, :width] = jnp.where(low, a, b)
                grads[rel * rows : (rel + 1) * rows, width:] = jnp.where(low, b, a)

        @pl.when(step < steps)
        def _():
            for rel in range(groups):
                hidden[rel * rows : (rel + 1) * rows, :] = first[rel][...]

        @pl.when(step >= steps)
        def _():
            for rel in range(groups):
                hidden[rel * rows : (rel + 1) * rows, :] = second[rel][...]

        total = lax.dot_general(
            hidden[...], grads[...], (((0,), (0,)), ((), ())), preferred_element_type=jnp.float32
        )
        out[...] = keep_blocks(total, lambda i, j: flags[step * blocks + i, j]).astype(out.dtype)

    first_spec = pl.BlockSpec((rows, tile), lambda j, *_: (0, jnp.minimum(j, steps - 1)))
    second_spec = pl.BlockSpec((rows, tile), lambda j, *_: (0, jnp.maximum(j - steps, 0)))
    return pl.pallas_call(
        kernel,
        grid_spec=pltpu.PrefetchScalarGridSpec(
            num_scalar_prefetch=2,
            grid=(2 * steps,),
            in_specs=[first_spec] * groups + [second_spec] * groups + [full, full],
            out_specs=pl.BlockSpec((tile, 2 * width), lambda j, *_: (j, 0)),
            scratch_shapes=[
                pltpu.VMEM((groups * rows, tile), jnp.bfloat16),
                pltpu.VMEM((groups * rows, 2 * width), jnp.bfloat16),
            ],
        ),
        out_shape=jax.ShapeDtypeStruct((2 * span, 2 * width), jnp.bfloat16),
        compiler_params=pltpu.CompilerParams(vmem_limit_bytes=VMEM_BYTES),
        cost_estimate=pl.CostEstimate(
            flops=8 * groups * rows * span * width,
            bytes_accessed=4 * groups * rows * (span + width) + 8 * span * width,
            transcendentals=0,
        ),
    )(place, flags, *halves[0], *halves[1], own, other)


def per_device(
    tokens, out_grad, gate_weight, up_weight, down_weight, gate_mask, up_mask, down_mask
):
    n_f = lax.axis_size("fsdp")
    n_t = lax.axis_size("tensor")
    assert n_t == 2 * n_f and n_f & (n_f - 1) == 0
    bits = n_f.bit_length() - 1
    rows, width = tokens.shape
    f_index = lax.axis_index("fsdp")
    t_index = lax.axis_index("tensor")
    owner, core = t_index // 2, t_index % 2
    place = jnp.stack([owner ^ f_index, core]).astype(jnp.int32)
    swap = [
        (f * n_t + 2 * a + c, a * n_t + 2 * f + c)
        for f in range(n_f)
        for a in range(n_f)
        for c in range(2)
    ]
    bit_orders = (tuple(range(bits)), tuple(reversed(range(bits))))

    def group_order(bit_order):
        order = []
        for i in range(n_f):
            order.append(sum(((i >> (bits - 1 - p)) & 1) << b for p, b in enumerate(bit_order)))
        return tuple(order)

    def across(x, bit):
        return lax.ppermute(x, "fsdp", [(f, f ^ (1 << bit)) for f in range(n_f)])

    def along(x, k):
        return lax.ppermute(x, "tensor", [(t, t ^ (2 * k)) for t in range(n_t)])

    def exchange(x):
        return lax.ppermute(x, "tensor", [(t, t ^ 1) for t in range(n_t)])

    def owner_columns(x):
        moved = lax.ppermute(x, AXES, swap)
        own = jnp.stack([moved] + [along(moved, k) for k in range(1, n_f)])
        return own, exchange(own)

    def own_flags(mask, weight, row, col):
        rb, cb = weight.shape[0] // BLOCK, weight.shape[1] // BLOCK
        return lax.dynamic_slice(mask, (row * rb, col * cb), (rb, cb))

    gate_flags = own_flags(gate_mask, gate_weight, f_index, t_index)
    up_flags = own_flags(up_mask, up_weight, f_index, t_index)
    down_flags = own_flags(down_mask, down_weight, t_index, f_index)

    def owner_sum(kept, sent, bit_order):
        for bit in bit_order:
            total = kept + across(sent, bit).astype(jnp.float32)
            groups = total.shape[0]
            kept, sent = total[: groups // 2], total[groups // 2 :].astype(jnp.bfloat16)
        return total[0]

    def gathered(piece, bit_order):
        held = {0: piece}
        for bit in bit_order:
            for rel in list(held):
                held[rel | 1 << bit] = across(held[rel], bit)
        return [held[rel] for rel in range(n_f)]

    def forward(columns, weight, flags, transposed):
        sums = []
        for half in range(2):
            kept, sent = forward_half(
                place, flags, *columns, weight, group_order(bit_orders[half]), half, transposed
            )
            sums.append(owner_sum(kept, sent, bit_orders[half]))
        return sums

    x_cols = owner_columns(tokens)
    g_cols = owner_columns(out_grad)
    gate_pre = forward(x_cols, gate_weight, gate_flags, False)
    up_pre = forward(x_cols, up_weight, up_flags, False)
    hidden_grad = forward(g_cols, down_weight, down_flags, True)

    gate_pieces, up_pieces, hidden_pieces = [], [], []
    for half in range(2):
        v, u, d = gate_pre[half], up_pre[half], hidden_grad[half]
        sig = jax.nn.sigmoid(v)
        act = v * sig
        hidden = (act * u).astype(jnp.bfloat16)
        gate_grad = (d * u * (sig * (1.0 + v * (1.0 - sig)))).astype(jnp.bfloat16)
        up_grad = (d * act).astype(jnp.bfloat16)
        gate_pieces += gathered(gate_grad, bit_orders[half])
        up_pieces += gathered(up_grad, bit_orders[half])
        hidden_pieces.append(gathered(hidden, bit_orders[half]))

    def side(own_side):
        return input_side(
            place,
            gate_flags,
            up_flags,
            gate_pieces + up_pieces,
            gate_weight,
            up_weight,
            n_f,
            width,
            own_side,
        )

    from_core = exchange(side(False))
    chip_sum = side(True) + from_core.astype(jnp.float32)
    to_send = chip_sum.astype(jnp.bfloat16)
    total = chip_sum[0]
    for k in range(1, n_f):
        total = total + along(to_send[k], k).astype(jnp.float32)
    input_grad = lax.ppermute(total.astype(jnp.bfloat16), AXES, swap)
    down_grad = down_product(place, down_flags, *g_cols, hidden_pieces)
    return (input_grad, down_grad)


def solution(mesh):
    return jax.shard_map(
        per_device,
        mesh=mesh,
        in_specs=(
            P("fsdp", "tensor"),
            P("fsdp", "tensor"),
            P("fsdp", "tensor"),
            P("fsdp", "tensor"),
            P("tensor", "fsdp"),
            P(),
            P(),
            P(),
        ),
        out_specs=(P("fsdp", "tensor"), P("tensor", "fsdp")),
        check_vma=False,
    )
```

```python
import functools

import jax
import jax.numpy as jnp
from jax import lax
from jax.experimental import pallas as pl
from jax.experimental.pallas import tpu as pltpu
from jax.sharding import PartitionSpec as P

BLOCK = 128
VMEM_BYTES = 48 * 1024 * 1024


def keep_blocks(weight, flag_of):
    rows = []
    for i in range(weight.shape[0] // BLOCK):
        row = []
        for j in range(weight.shape[1] // BLOCK):
            block = weight[i * BLOCK : (i + 1) * BLOCK, j * BLOCK : (j + 1) * BLOCK]
            row.append(jnp.where(flag_of(i, j) == 1, block, jnp.zeros_like(block)))
        rows.append(jnp.concatenate(row, axis=1))
    return jnp.concatenate(rows, axis=0)


def fill_columns(target, start, low, own, other):
    rows, width = own.shape
    target[start : start + rows, :width] = jnp.where(low, own, other)
    target[start : start + rows, width:] = jnp.where(low, other, own)


def forward_half(place, weights, all_flags, parts, order, half, transposed):
    groups, rows, width = parts[0][0].shape
    n_parts, n_weights = len(parts), len(weights)
    inner = 2 * width
    span = weights[0].shape[0 if transposed else 1] // 2
    tile = min(512, span)
    steps = span // tile
    blocks = tile // BLOCK
    group_rows = n_parts * rows

    def kernel(place, *refs):
        flags, refs = refs[:n_weights], refs[n_weights:]
        columns, refs = refs[: 2 * n_parts], refs[2 * n_parts :]
        blocks_in, (kept, sent, x_all) = refs[:n_weights], refs[n_weights:]
        step = pl.program_id(0)

        @pl.when(step == 0)
        def _():
            low = place[0] == 0
            for i in range(groups):
                for p in range(n_parts):
                    g, start = order[i], i * group_rows + p * rows
                    fill_columns(x_all, start, low, columns[2 * p][g], columns[2 * p + 1][g])

        first = (half * steps + step) * blocks
        for w in range(n_weights):
            flag = flags[w]
            if transposed:
                masked = keep_blocks(blocks_in[w][...], lambda i, j: flag[first + i, j])
                dims = (((1,), (1,)), ((), ()))
            else:
                masked = keep_blocks(blocks_in[w][...], lambda i, j: flag[i, first + j])
                dims = (((1,), (0,)), ((), ()))
            part = lax.dot_general(x_all[...], masked, dims, preferred_element_type=jnp.float32)
            part = part.reshape(groups, group_rows, tile)
            kept[:, w] = part[: groups // 2]
            sent[:, w] = part[groups // 2 :].astype(jnp.bfloat16)

    full = pl.BlockSpec((groups, rows, width), lambda j, *_: (0, 0, 0))
    if transposed:
        weight_spec = pl.BlockSpec((tile, inner), lambda j, *_: (half * steps + j, 0))
    else:
        weight_spec = pl.BlockSpec((inner, tile), lambda j, *_: (0, half * steps + j))
    out_spec = pl.BlockSpec((groups // 2, n_weights, group_rows, tile), lambda j, *_: (0, 0, 0, j))
    shape = (groups // 2, n_weights, group_rows, span)
    return pl.pallas_call(
        kernel,
        grid_spec=pltpu.PrefetchScalarGridSpec(
            num_scalar_prefetch=1 + n_weights,
            grid=(steps,),
            in_specs=[full] * (2 * n_parts) + [weight_spec] * n_weights,
            out_specs=[out_spec, out_spec],
            scratch_shapes=[pltpu.VMEM((groups * group_rows, inner), jnp.bfloat16)],
        ),
        out_shape=[
            jax.ShapeDtypeStruct(shape, jnp.float32),
            jax.ShapeDtypeStruct(shape, jnp.bfloat16),
        ],
        compiler_params=pltpu.CompilerParams(vmem_limit_bytes=VMEM_BYTES),
        cost_estimate=pl.CostEstimate(
            flops=2 * groups * group_rows * inner * span * n_weights,
            bytes_accessed=2 * inner * (groups * group_rows + n_weights * span)
            + 3 * groups * group_rows * span * n_weights,
            transcendentals=0,
        ),
    )(place, *all_flags, *[x for part in parts for x in part], *weights)


def input_side(place, gate_flags, up_flags, pieces, gate, up, width, own_side):
    groups = len(pieces) // 2
    _, rows, span = pieces[0].shape
    tile = min(256, width)
    tiles = width // tile
    blocks = tile // BLOCK

    def side_of(place):
        return place[0] if own_side else 1 - place[0]

    def kernel(place, gate_flags, up_flags, *refs):
        held, (gate, up, out, stacked) = refs[: 2 * groups], refs[2 * groups :]
        step = pl.program_id(0)

        @pl.when(step == 0)
        def _():
            for half in range(2):
                for rel in range(groups):
                    piece = held[half * groups + rel]
                    for which in range(2):
                        start = (2 * which + half) * span
                        stacked[rel, :, start : start + span] = piece[which]

        first = (side_of(place) * tiles + step) * blocks
        grads = stacked[...].reshape(groups * rows, 4 * span)
        dims = (((1,), (1,)), ((), ()))
        gate_kept = keep_blocks(gate[...], lambda i, j: gate_flags[first + i, j])
        up_kept = keep_blocks(up[...], lambda i, j: up_flags[first + i, j])
        total = lax.dot_general(
            grads[:, : 2 * span], gate_kept, dims, preferred_element_type=jnp.float32
        ) + lax.dot_general(
            grads[:, 2 * span :], up_kept, dims, preferred_element_type=jnp.float32
        )
        out[...] = total.reshape(groups, rows, tile).astype(out.dtype)

    whole = pl.BlockSpec((2, rows, span), lambda j, *_: (0, 0, 0))
    weight_spec = pl.BlockSpec(
        (tile, gate.shape[1]), lambda j, place, *_: (side_of(place) * tiles + j, 0)
    )
    return pl.pallas_call(
        kernel,
        grid_spec=pltpu.PrefetchScalarGridSpec(
            num_scalar_prefetch=3,
            grid=(tiles,),
            in_specs=[whole] * len(pieces) + [weight_spec, weight_spec],
            out_specs=pl.BlockSpec((groups, rows, tile), lambda j, *_: (0, 0, j)),
            scratch_shapes=[pltpu.VMEM((groups, rows, 4 * span), jnp.bfloat16)],
        ),
        out_shape=jax.ShapeDtypeStruct(
            (groups, rows, width), jnp.float32 if own_side else jnp.bfloat16
        ),
        compiler_params=pltpu.CompilerParams(vmem_limit_bytes=VMEM_BYTES),
        cost_estimate=pl.CostEstimate(
            flops=2 * groups * rows * 4 * span * width,
            bytes_accessed=8 * span * (groups * rows + width) + 4 * groups * rows * width,
            transcendentals=0,
        ),
    )(place, gate_flags, up_flags, *pieces, gate, up)


def down_product(place, flags, parts, halves):
    groups, rows, width = parts[0][0].shape
    n_parts = len(parts)
    group_rows = n_parts * rows
    span = halves[0][0].shape[1]
    tile = min(512, span)
    steps = span // tile
    blocks = tile // BLOCK

    def kernel(place, flags, *refs):
        first, second = refs[:groups], refs[groups : 2 * groups]
        columns, refs = refs[2 * groups : 2 * groups + 2 * n_parts], refs[2 * groups + 2 * n_parts :]
        out, hidden, grads = refs
        step = pl.program_id(0)

        @pl.when(step == 0)
        def _():
            low = place[0] == 0
            for rel in range(groups):
                for p in range(n_parts):
                    start = rel * group_rows + p * rows
                    fill_columns(grads, start, low, columns[2 * p][rel], columns[2 * p + 1][rel])

        @pl.when(step < steps)
        def _():
            for rel in range(groups):
                hidden[rel * group_rows : (rel + 1) * group_rows, :] = first[rel][...]

        @pl.when(step >= steps)
        def _():
            for rel in range(groups):
                hidden[rel * group_rows : (rel + 1) * group_rows, :] = second[rel][...]

        total = lax.dot_general(
            hidden[...], grads[...], (((0,), (0,)), ((), ())), preferred_element_type=jnp.float32
        )
        out[...] = keep_blocks(total, lambda i, j: flags[step * blocks + i, j]).astype(out.dtype)

    full = pl.BlockSpec((groups, rows, width), lambda j, *_: (0, 0, 0))
    first_spec = pl.BlockSpec((group_rows, tile), lambda j, *_: (0, jnp.minimum(j, steps - 1)))
    second_spec = pl.BlockSpec((group_rows, tile), lambda j, *_: (0, jnp.maximum(j - steps, 0)))
    return pl.pallas_call(
        kernel,
        grid_spec=pltpu.PrefetchScalarGridSpec(
            num_scalar_prefetch=2,
            grid=(2 * steps,),
            in_specs=[first_spec] * groups + [second_spec] * groups + [full] * (2 * n_parts),
            out_specs=pl.BlockSpec((tile, 2 * width), lambda j, *_: (j, 0)),
            scratch_shapes=[
                pltpu.VMEM((groups * group_rows, tile), jnp.bfloat16),
                pltpu.VMEM((groups * group_rows, 2 * width), jnp.bfloat16),
            ],
        ),
        out_shape=jax.ShapeDtypeStruct((2 * span, 2 * width), jnp.bfloat16),
        compiler_params=pltpu.CompilerParams(vmem_limit_bytes=VMEM_BYTES),
        cost_estimate=pl.CostEstimate(
            flops=8 * groups * group_rows * span * width,
            bytes_accessed=4 * groups * group_rows * (span + width) + 8 * span * width,
            transcendentals=0,
        ),
    )(place, flags, *halves[0], *halves[1], *[x for part in parts for x in part])


def after(x, *others):
    return lax.optimization_barrier((x, others))[0]


def per_device(
    tokens, out_grad, gate_weight, up_weight, down_weight, gate_mask, up_mask, down_mask
):
    n_f = lax.axis_size("fsdp")
    n_t = lax.axis_size("tensor")
    assert n_t == 2 * n_f and n_f & (n_f - 1) == 0
    bits = n_f.bit_length() - 1
    rows, width = tokens.shape
    sub = rows // n_f
    f_index = lax.axis_index("fsdp")
    t_index = lax.axis_index("tensor")
    plane = t_index // 2
    place = jnp.reshape(t_index % 2, (1,)).astype(jnp.int32)
    bit_orders = (tuple(range(bits)), tuple(reversed(range(bits))))

    def group_order(bit_order):
        order = []
        for i in range(n_f):
            order.append(sum(((i >> (bits - 1 - p)) & 1) << b for p, b in enumerate(bit_order)))
        return tuple(order)

    def across(x, k):
        return lax.ppermute(x, "fsdp", [(f, f ^ k) for f in range(n_f)])

    def along(x, k):
        return lax.ppermute(x, "tensor", [(t, t ^ (2 * k)) for t in range(n_t)])

    def exchange(x):
        return lax.ppermute(x, "tensor", [(t, t ^ 1) for t in range(n_t)])

    def reordered(x, index):
        for b in range(bits):
            pairs = x.reshape(-1, 2, 1 << b, *x.shape[1:])
            flipped = pairs[:, ::-1].reshape(x.shape)
            x = jnp.where((index >> b) & 1 == 1, flipped, x)
        return x

    def swapped(x, move):
        return jnp.stack([x[0]] + [move(x[k], k) for k in range(1, n_f)])

    def own_flags(mask, weight, row, col):
        rb, cb = weight.shape[0] // BLOCK, weight.shape[1] // BLOCK
        return lax.dynamic_slice(mask, (row * rb, col * cb), (rb, cb))

    gate_flags = own_flags(gate_mask, gate_weight, f_index, t_index)
    up_flags = own_flags(up_mask, up_weight, f_index, t_index)
    down_flags = own_flags(down_mask, down_weight, t_index, f_index)

    both = jnp.stack([tokens.reshape(n_f, sub, width), out_grad.reshape(n_f, sub, width)], axis=1)
    both = swapped(reordered(both, plane), along)
    both = swapped(reordered(both, plane ^ f_index), across)
    x_own, g_own = both[:, 0], both[:, 1]

    def part_of(pieces):
        own = jnp.concatenate(pieces, axis=1)
        return own, exchange(own)

    def owner_sum(kept, sent, bit_order):
        for bit in bit_order:
            total = kept + across(sent, 1 << bit).astype(jnp.float32)
            groups = total.shape[0]
            kept, sent = total[: groups // 2], total[groups // 2 :].astype(jnp.bfloat16)
        return total[0]

    def gathered(piece, bit_order):
        held = {0: piece}
        for bit in bit_order:
            for rel in list(held):
                held[rel | 1 << bit] = across(held[rel], 1 << bit)
        return [held[rel] for rel in range(n_f)]

    def forward(parts, weights, flags, transposed, previous=()):
        products = []
        for half in range(2):
            turn = after(place, *previous)
            order = group_order(bit_orders[half])
            products.append(forward_half(turn, weights, flags, parts, order, half, transposed))
            previous = products[-1]
        return products

    def sums(products):
        return [owner_sum(*products[half], bit_orders[half]) for half in range(2)]

    projections = ([gate_weight, up_weight], [gate_flags, up_flags], False)
    near = [x_own] + [along(x_own, k) for k in range(1, n_f // 2)]
    far_own = after(x_own, near[-1])
    far = [along(far_own, k) for k in range(n_f // 2, n_f)]
    part_a = part_of(near)
    products_a = forward([part_a], *projections)
    part_b = part_of(far)
    products_b = forward([part_b], *projections, products_a[1])
    g_start = after(g_own, far[-1], products_a[1])
    g_parts = [part_of([g_start] + [along(g_start, k) for k in range(1, n_f)])]
    products_g = forward(g_parts, [down_weight], [down_flags], True, products_b[1])
    pre = [sums(products_a), sums(products_b)]
    hidden_grad = sums(products_g)

    part_rows = rows // 2
    grads, hidden = [[], []], [[], []]
    for half in range(2):
        for p in range(2):
            v, u = pre[p][half][0], pre[p][half][1]
            d = hidden_grad[half][0, p * part_rows : (p + 1) * part_rows]
            sig = jax.nn.sigmoid(v)
            act = v * sig
            hidden[half].append((act * u).astype(jnp.bfloat16))
            gate_grad = d * u * (sig * (1.0 + v * (1.0 - sig)))
            grads[p].append(jnp.stack([gate_grad, d * act]).astype(jnp.bfloat16))

    def chip_sum(pieces, *previous):
        args = (gate_flags, up_flags, pieces, gate_weight, up_weight, width)
        for_core = input_side(after(place, *previous), *args, False)
        mine = input_side(after(place, for_core), *args, True)
        return mine + exchange(for_core).astype(jnp.float32), mine

    def both_halves(p):
        return [x for half in range(2) for x in gathered(grads[p][half], bit_orders[half])]

    def plane_sums(part, first):
        return [
            along(part[:, i * sub : (i + 1) * sub].astype(jnp.bfloat16), first + i)
            for i in range(part.shape[1] // sub)
            if first + i
        ]

    hidden_pieces = [
        gathered(jnp.concatenate(hidden[half]), bit_orders[half]) for half in range(2)
    ]
    far_part, far_mine = chip_sum(
        both_halves(1), *[x for held in hidden_pieces for x in held[:-1]]
    )
    far_sums = plane_sums(far_part, n_f // 2)
    near_part, near_mine = chip_sum(both_halves(0), far_mine)
    near_sums = plane_sums(near_part, 0)
    down_grad = down_product(after(place, near_mine), down_flags, g_parts, hidden_pieces)
    near_sums[-1] = after(near_sums[-1], down_grad)
    total = near_part[:, :sub]
    for received in far_sums + near_sums:
        total = total + received.astype(jnp.float32)
    back = swapped(total.astype(jnp.bfloat16), across)
    back = swapped(reordered(back, plane ^ f_index), along)
    input_grad = reordered(back, plane).reshape(rows, width)
    return (input_grad, down_grad)


def solution(mesh):
    return jax.shard_map(
        per_device,
        mesh=mesh,
        in_specs=(
            P("fsdp", "tensor"),
            P("fsdp", "tensor"),
            P("fsdp", "tensor"),
            P("fsdp", "tensor"),
            P("tensor", "fsdp"),
            P(),
            P(),
            P(),
        ),
        out_specs=(P("fsdp", "tensor"), P("tensor", "fsdp")),
        check_vma=False,
    )
```

```python
import functools

import jax
import jax.numpy as jnp
from jax import lax
from jax.experimental import pallas as pl
from jax.experimental.pallas import tpu as pltpu
from jax.sharding import PartitionSpec as P

BLOCK = 128
VMEM_BYTES = 28 * 1024 * 1024


def keep_blocks(weight, flag_of):
    rows = []
    for i in range(weight.shape[0] // BLOCK):
        row = []
        for j in range(weight.shape[1] // BLOCK):
            block = weight[i * BLOCK : (i + 1) * BLOCK, j * BLOCK : (j + 1) * BLOCK]
            row.append(jnp.where(flag_of(i, j) == 1, block, jnp.zeros_like(block)))
        rows.append(jnp.concatenate(row, axis=1))
    return jnp.concatenate(rows, axis=0)


def fill_columns(target, start, low, own, other):
    rows, width = own.shape
    target[start : start + rows, :width] = jnp.where(low, own, other)
    target[start : start + rows, width:] = jnp.where(low, other, own)


def forward_half(place, weights, all_flags, parts, order, half, transposed):
    groups, rows, width = parts[0][0].shape
    n_parts, n_weights = len(parts), len(weights)
    inner = 2 * width
    span = weights[0].shape[0 if transposed else 1] // 2
    tile = min(512, span)
    steps = span // tile
    blocks = tile // BLOCK
    group_rows = n_parts * rows

    def kernel(place, *refs):
        flags, refs = refs[:n_weights], refs[n_weights:]
        columns, refs = refs[: 2 * n_parts], refs[2 * n_parts :]
        blocks_in, (kept, sent, x_all) = refs[:n_weights], refs[n_weights:]
        step = pl.program_id(0)

        @pl.when(step == 0)
        def _():
            low = place[0] == 0
            for i in range(groups):
                for p in range(n_parts):
                    g, start = order[i], i * group_rows + p * rows
                    fill_columns(x_all, start, low, columns[2 * p][g], columns[2 * p + 1][g])

        first = (half * steps + step) * blocks
        for w in range(n_weights):
            flag = flags[w]
            if transposed:
                masked = keep_blocks(blocks_in[w][...], lambda i, j: flag[first + i, j])
                dims = (((1,), (1,)), ((), ()))
            else:
                masked = keep_blocks(blocks_in[w][...], lambda i, j: flag[i, first + j])
                dims = (((1,), (0,)), ((), ()))
            part = lax.dot_general(x_all[...], masked, dims, preferred_element_type=jnp.float32)
            part = part.reshape(groups, group_rows, tile)
            kept[:, w] = part[: groups // 2]
            sent[:, w] = part[groups // 2 :].astype(jnp.bfloat16)

    full = pl.BlockSpec((groups, rows, width), lambda j, *_: (0, 0, 0))
    if transposed:
        weight_spec = pl.BlockSpec((tile, inner), lambda j, *_: (half * steps + j, 0))
    else:
        weight_spec = pl.BlockSpec((inner, tile), lambda j, *_: (0, half * steps + j))
    out_spec = pl.BlockSpec((groups // 2, n_weights, group_rows, tile), lambda j, *_: (0, 0, 0, j))
    shape = (groups // 2, n_weights, group_rows, span)
    return pl.pallas_call(
        kernel,
        grid_spec=pltpu.PrefetchScalarGridSpec(
            num_scalar_prefetch=1 + n_weights,
            grid=(steps,),
            in_specs=[full] * (2 * n_parts) + [weight_spec] * n_weights,
            out_specs=[out_spec, out_spec],
            scratch_shapes=[pltpu.VMEM((groups * group_rows, inner), jnp.bfloat16)],
        ),
        out_shape=[
            jax.ShapeDtypeStruct(shape, jnp.float32),
            jax.ShapeDtypeStruct(shape, jnp.bfloat16),
        ],
        compiler_params=pltpu.CompilerParams(vmem_limit_bytes=VMEM_BYTES),
        cost_estimate=pl.CostEstimate(
            flops=2 * groups * group_rows * inner * span * n_weights,
            bytes_accessed=2 * inner * (groups * group_rows + n_weights * span)
            + 3 * groups * group_rows * span * n_weights,
            transcendentals=0,
        ),
    )(place, *all_flags, *[x for part in parts for x in part], *weights)


def input_side(place, gate_flags, up_flags, pieces, gate, up, width, own_side):
    groups = len(pieces) // 2
    _, rows, span = pieces[0].shape
    tile = min(256, width)
    tiles = width // tile
    blocks = tile // BLOCK

    def side_of(place):
        return place[0] if own_side else 1 - place[0]

    def kernel(place, gate_flags, up_flags, *refs):
        held, (gate, up, out, stacked) = refs[: 2 * groups], refs[2 * groups :]
        step = pl.program_id(0)

        @pl.when(step == 0)
        def _():
            for half in range(2):
                for rel in range(groups):
                    piece = held[half * groups + rel]
                    for which in range(2):
                        start = (2 * which + half) * span
                        stacked[rel, :, start : start + span] = piece[which]

        first = (side_of(place) * tiles + step) * blocks
        grads = stacked[...].reshape(groups * rows, 4 * span)
        dims = (((1,), (1,)), ((), ()))
        gate_kept = keep_blocks(gate[...], lambda i, j: gate_flags[first + i, j])
        up_kept = keep_blocks(up[...], lambda i, j: up_flags[first + i, j])
        total = lax.dot_general(
            grads[:, : 2 * span], gate_kept, dims, preferred_element_type=jnp.float32
        ) + lax.dot_general(
            grads[:, 2 * span :], up_kept, dims, preferred_element_type=jnp.float32
        )
        out[...] = total.reshape(groups, rows, tile).astype(out.dtype)

    whole = pl.BlockSpec((2, rows, span), lambda j, *_: (0, 0, 0))
    weight_spec = pl.BlockSpec(
        (tile, gate.shape[1]), lambda j, place, *_: (side_of(place) * tiles + j, 0)
    )
    return pl.pallas_call(
        kernel,
        grid_spec=pltpu.PrefetchScalarGridSpec(
            num_scalar_prefetch=3,
            grid=(tiles,),
            in_specs=[whole] * len(pieces) + [weight_spec, weight_spec],
            out_specs=pl.BlockSpec((groups, rows, tile), lambda j, *_: (0, 0, j)),
            scratch_shapes=[pltpu.VMEM((groups, rows, 4 * span), jnp.bfloat16)],
        ),
        out_shape=jax.ShapeDtypeStruct(
            (groups, rows, width), jnp.float32 if own_side else jnp.bfloat16
        ),
        compiler_params=pltpu.CompilerParams(vmem_limit_bytes=VMEM_BYTES),
        cost_estimate=pl.CostEstimate(
            flops=2 * groups * rows * 4 * span * width,
            bytes_accessed=8 * span * (groups * rows + width) + 4 * groups * rows * width,
            transcendentals=0,
        ),
    )(place, gate_flags, up_flags, *pieces, gate, up)


def down_product(place, flags, parts, halves):
    groups, rows, width = parts[0][0].shape
    n_parts = len(parts)
    group_rows = n_parts * rows
    span = halves[0][0].shape[1]
    tile = min(512, span)
    steps = span // tile
    blocks = tile // BLOCK

    def kernel(place, flags, *refs):
        first, second = refs[:groups], refs[groups : 2 * groups]
        columns, refs = refs[2 * groups : 2 * groups + 2 * n_parts], refs[2 * groups + 2 * n_parts :]
        out, hidden, grads = refs
        step = pl.program_id(0)

        @pl.when(step == 0)
        def _():
            low = place[0] == 0
            for rel in range(groups):
                for p in range(n_parts):
                    start = rel * group_rows + p * rows
                    fill_columns(grads, start, low, columns[2 * p][rel], columns[2 * p + 1][rel])

        @pl.when(step < steps)
        def _():
            for rel in range(groups):
                hidden[rel * group_rows : (rel + 1) * group_rows, :] = first[rel][...]

        @pl.when(step >= steps)
        def _():
            for rel in range(groups):
                hidden[rel * group_rows : (rel + 1) * group_rows, :] = second[rel][...]

        total = lax.dot_general(
            hidden[...], grads[...], (((0,), (0,)), ((), ())), preferred_element_type=jnp.float32
        )
        out[...] = keep_blocks(total, lambda i, j: flags[step * blocks + i, j]).astype(out.dtype)

    full = pl.BlockSpec((groups, rows, width), lambda j, *_: (0, 0, 0))
    first_spec = pl.BlockSpec((group_rows, tile), lambda j, *_: (0, jnp.minimum(j, steps - 1)))
    second_spec = pl.BlockSpec((group_rows, tile), lambda j, *_: (0, jnp.maximum(j - steps, 0)))
    return pl.pallas_call(
        kernel,
        grid_spec=pltpu.PrefetchScalarGridSpec(
            num_scalar_prefetch=2,
            grid=(2 * steps,),
            in_specs=[first_spec] * groups + [second_spec] * groups + [full] * (2 * n_parts),
            out_specs=pl.BlockSpec((tile, 2 * width), lambda j, *_: (j, 0)),
            scratch_shapes=[
                pltpu.VMEM((groups * group_rows, tile), jnp.bfloat16),
                pltpu.VMEM((groups * group_rows, 2 * width), jnp.bfloat16),
            ],
        ),
        out_shape=jax.ShapeDtypeStruct((2 * span, 2 * width), jnp.bfloat16),
        compiler_params=pltpu.CompilerParams(vmem_limit_bytes=VMEM_BYTES),
        cost_estimate=pl.CostEstimate(
            flops=8 * groups * group_rows * span * width,
            bytes_accessed=4 * groups * group_rows * (span + width) + 8 * span * width,
            transcendentals=0,
        ),
    )(place, flags, *halves[0], *halves[1], *[x for part in parts for x in part])


def after(x, *others):
    return lax.optimization_barrier((x, others))[0]


def per_device(
    tokens, out_grad, gate_weight, up_weight, down_weight, gate_mask, up_mask, down_mask
):
    n_f = lax.axis_size("fsdp")
    n_t = lax.axis_size("tensor")
    assert n_t == 2 * n_f and n_f & (n_f - 1) == 0
    bits = n_f.bit_length() - 1
    rows, width = tokens.shape
    sub = rows // n_f
    f_index = lax.axis_index("fsdp")
    t_index = lax.axis_index("tensor")
    plane = t_index // 2
    place = jnp.reshape(t_index % 2, (1,)).astype(jnp.int32)
    bit_orders = (tuple(range(bits)), tuple(reversed(range(bits))))

    def group_order(bit_order):
        order = []
        for i in range(n_f):
            order.append(sum(((i >> (bits - 1 - p)) & 1) << b for p, b in enumerate(bit_order)))
        return tuple(order)

    def across(x, k):
        return lax.ppermute(x, "fsdp", [(f, f ^ k) for f in range(n_f)])

    def along(x, k):
        return lax.ppermute(x, "tensor", [(t, t ^ (2 * k)) for t in range(n_t)])

    def exchange(x):
        return lax.ppermute(x, "tensor", [(t, t ^ 1) for t in range(n_t)])

    def reordered(x, index):
        for b in range(bits):
            pairs = x.reshape(-1, 2, 1 << b, *x.shape[1:])
            flipped = pairs[:, ::-1].reshape(x.shape)
            x = jnp.where((index >> b) & 1 == 1, flipped, x)
        return x

    def swapped(x, move):
        return jnp.stack([x[0]] + [move(x[k], k) for k in range(1, n_f)])

    def own_flags(mask, weight, row, col):
        rb, cb = weight.shape[0] // BLOCK, weight.shape[1] // BLOCK
        return lax.dynamic_slice(mask, (row * rb, col * cb), (rb, cb))

    gate_flags = own_flags(gate_mask, gate_weight, f_index, t_index)
    up_flags = own_flags(up_mask, up_weight, f_index, t_index)
    down_flags = own_flags(down_mask, down_weight, t_index, f_index)

    both = jnp.stack([tokens.reshape(n_f, sub, width), out_grad.reshape(n_f, sub, width)], axis=1)
    both = swapped(reordered(both, plane), along)
    both = swapped(reordered(both, plane ^ f_index), across)
    x_own, g_own = both[:, 0], both[:, 1]

    def part_of(pieces):
        own = jnp.concatenate(pieces, axis=1)
        return own, exchange(own)

    def owner_sum(kept, sent, bit_order):
        for bit in bit_order:
            total = kept + across(sent, 1 << bit).astype(jnp.float32)
            groups = total.shape[0]
            kept, sent = total[: groups // 2], total[groups // 2 :].astype(jnp.bfloat16)
        return total[0]

    def gathered(piece, bit_order):
        held = {0: piece}
        for bit in bit_order:
            for rel in list(held):
                held[rel | 1 << bit] = across(held[rel], 1 << bit)
        return [held[rel] for rel in range(n_f)]

    def forward(parts, weights, flags, transposed, previous=()):
        products = []
        for half in range(2):
            turn = after(place, *previous)
            order = group_order(bit_orders[half])
            products.append(forward_half(turn, weights, flags, parts, order, half, transposed))
            previous = products[-1]
        return products

    def sums(products):
        return [owner_sum(*products[half], bit_orders[half]) for half in range(2)]

    projections = ([gate_weight, up_weight], [gate_flags, up_flags], False)
    near = [x_own] + [along(x_own, k) for k in range(1, n_f // 2)]
    far_own = after(x_own, near[-1])
    far = [along(far_own, k) for k in range(n_f // 2, n_f)]
    part_a = part_of(near)
    products_a = forward([part_a], *projections)
    part_b = part_of(far)
    products_b = forward([part_b], *projections, products_a[1])
    g_start = after(g_own, far[-1], products_a[1])
    g_parts = [part_of([g_start] + [along(g_start, k) for k in range(1, n_f)])]
    products_g = forward(g_parts, [down_weight], [down_flags], True, products_b[1])
    pre = [sums(products_a), sums(products_b)]
    hidden_grad = sums(products_g)

    part_rows = rows // 2
    grads, hidden = [[], []], [[], []]
    for half in range(2):
        for p in range(2):
            v, u = pre[p][half][0], pre[p][half][1]
            d = hidden_grad[half][0, p * part_rows : (p + 1) * part_rows]
            sig = jax.nn.sigmoid(v)
            act = v * sig
            hidden[half].append((act * u).astype(jnp.bfloat16))
            gate_grad = d * u * (sig * (1.0 + v * (1.0 - sig)))
            grads[p].append(jnp.stack([gate_grad, d * act]).astype(jnp.bfloat16))

    def chip_sum(pieces, *previous):
        args = (gate_flags, up_flags, pieces, gate_weight, up_weight, width)
        for_core = input_side(after(place, *previous), *args, False)
        mine = input_side(after(place, for_core), *args, True)
        return mine + exchange(for_core).astype(jnp.float32), mine

    def both_halves(p):
        return [x for half in range(2) for x in gathered(grads[p][half], bit_orders[half])]

    hidden_pieces = [
        gathered(jnp.concatenate(hidden[half]), bit_orders[half]) for half in range(2)
    ]
    far_part, far_mine = chip_sum(
        both_halves(1), *[x for held in hidden_pieces for x in held[:-1]]
    )
    near_part, near_mine = chip_sum(both_halves(0), far_mine)
    def to_rows(part):
        part = part.astype(jnp.bfloat16)
        terms = [part[0]] + [across(part[m], m) for m in range(1, n_f)]
        for b in range(bits):
            odd = ((plane ^ f_index) >> b) & 1 == 1
            terms = [jnp.where(odd, terms[i ^ (1 << b)], x) for i, x in enumerate(terms)]
        return terms

    terms = [jnp.concatenate(x) for x in zip(to_rows(near_part), to_rows(far_part))]
    total = jnp.zeros((n_f, sub, width), jnp.float32)
    for k in range(n_f):
        term = along(terms[k], k) if k else terms[k]
        axes = [bits - 1 - b for b in range(bits) if (k >> b) & 1]
        flipped = jnp.flip(term.reshape((2,) * bits + (sub, width)), axes)
        total = total + flipped.reshape(n_f, sub, width).astype(jnp.float32)
    input_grad = reordered(total.astype(jnp.bfloat16), plane).reshape(rows, width)
    down_grad = down_product(after(place, *terms), down_flags, g_parts, hidden_pieces)
    return (input_grad, down_grad)


def solution(mesh):
    return jax.shard_map(
        per_device,
        mesh=mesh,
        in_specs=(
            P("fsdp", "tensor"),
            P("fsdp", "tensor"),
            P("fsdp", "tensor"),
            P("fsdp", "tensor"),
            P("tensor", "fsdp"),
            P(),
            P(),
            P(),
        ),
        out_specs=(P("fsdp", "tensor"), P("tensor", "fsdp")),
        check_vma=False,
    )
```

```python
import functools

import jax
import jax.numpy as jnp
from jax import lax
from jax.experimental import pallas as pl
from jax.experimental.pallas import tpu as pltpu
from jax.sharding import PartitionSpec as P

BLOCK = 128
VMEM_BYTES = 28 * 1024 * 1024


def keep_blocks(weight, flag_of):
    rows = []
    for i in range(weight.shape[0] // BLOCK):
        row = []
        for j in range(weight.shape[1] // BLOCK):
            block = weight[i * BLOCK : (i + 1) * BLOCK, j * BLOCK : (j + 1) * BLOCK]
            row.append(jnp.where(flag_of(i, j) == 1, block, jnp.zeros_like(block)))
        rows.append(jnp.concatenate(row, axis=1))
    return jnp.concatenate(rows, axis=0)


def fill_columns(target, start, low, own, other):
    rows, width = own.shape
    target[start : start + rows, :width] = jnp.where(low, own, other)
    target[start : start + rows, width:] = jnp.where(low, other, own)


def forward_half(place, weights, all_flags, parts, order, half, transposed):
    groups, rows, width = parts[0][0].shape
    n_parts, n_weights = len(parts), len(weights)
    inner = 2 * width
    span = weights[0].shape[0 if transposed else 1] // 2
    tile = min(512, span)
    steps = span // tile
    blocks = tile // BLOCK
    group_rows = n_parts * rows

    def kernel(place, *refs):
        flags, refs = refs[:n_weights], refs[n_weights:]
        columns, refs = refs[: 2 * n_parts], refs[2 * n_parts :]
        blocks_in, (kept, sent, x_all) = refs[:n_weights], refs[n_weights:]
        step = pl.program_id(0)

        @pl.when(step == 0)
        def _():
            low = place[0] == 0
            for i in range(groups):
                for p in range(n_parts):
                    g, start = order[i], i * group_rows + p * rows
                    fill_columns(x_all, start, low, columns[2 * p][g], columns[2 * p + 1][g])

        first = (half * steps + step) * blocks
        for w in range(n_weights):
            flag = flags[w]
            if transposed:
                masked = keep_blocks(blocks_in[w][...], lambda i, j: flag[first + i, j])
                dims = (((1,), (1,)), ((), ()))
            else:
                masked = keep_blocks(blocks_in[w][...], lambda i, j: flag[i, first + j])
                dims = (((1,), (0,)), ((), ()))
            part = lax.dot_general(x_all[...], masked, dims, preferred_element_type=jnp.float32)
            part = part.reshape(groups, group_rows, tile)
            kept[:, w] = part[: groups // 2].astype(jnp.bfloat16)
            sent[:, w] = part[groups // 2 :].astype(jnp.bfloat16)

    full = pl.BlockSpec((groups, rows, width), lambda j, *_: (0, 0, 0))
    if transposed:
        weight_spec = pl.BlockSpec((tile, inner), lambda j, *_: (half * steps + j, 0))
    else:
        weight_spec = pl.BlockSpec((inner, tile), lambda j, *_: (0, half * steps + j))
    out_spec = pl.BlockSpec((groups // 2, n_weights, group_rows, tile), lambda j, *_: (0, 0, 0, j))
    shape = (groups // 2, n_weights, group_rows, span)
    return pl.pallas_call(
        kernel,
        grid_spec=pltpu.PrefetchScalarGridSpec(
            num_scalar_prefetch=1 + n_weights,
            grid=(steps,),
            in_specs=[full] * (2 * n_parts) + [weight_spec] * n_weights,
            out_specs=[out_spec, out_spec],
            scratch_shapes=[pltpu.VMEM((groups * group_rows, inner), jnp.bfloat16)],
        ),
        out_shape=[
            jax.ShapeDtypeStruct(shape, jnp.bfloat16),
            jax.ShapeDtypeStruct(shape, jnp.bfloat16),
        ],
        compiler_params=pltpu.CompilerParams(vmem_limit_bytes=VMEM_BYTES),
        cost_estimate=pl.CostEstimate(
            flops=2 * groups * group_rows * inner * span * n_weights,
            bytes_accessed=2 * inner * (groups * group_rows + n_weights * span)
            + 3 * groups * group_rows * span * n_weights,
            transcendentals=0,
        ),
    )(place, *all_flags, *[x for part in parts for x in part], *weights)


def input_side(place, gate_flags, up_flags, pieces, gate, up, width, own_side):
    groups = len(pieces) // 2
    _, rows, span = pieces[0].shape
    tile = min(256, width)
    tiles = width // tile
    blocks = tile // BLOCK

    def side_of(place):
        return place[0] if own_side else 1 - place[0]

    def kernel(place, gate_flags, up_flags, *refs):
        held, (gate, up, out, stacked) = refs[: 2 * groups], refs[2 * groups :]
        step = pl.program_id(0)

        @pl.when(step == 0)
        def _():
            for half in range(2):
                for rel in range(groups):
                    piece = held[half * groups + rel]
                    for which in range(2):
                        start = (2 * which + half) * span
                        stacked[rel, :, start : start + span] = piece[which]

        first = (side_of(place) * tiles + step) * blocks
        grads = stacked[...].reshape(groups * rows, 4 * span)
        dims = (((1,), (1,)), ((), ()))
        gate_kept = keep_blocks(gate[...], lambda i, j: gate_flags[first + i, j])
        up_kept = keep_blocks(up[...], lambda i, j: up_flags[first + i, j])
        total = lax.dot_general(
            grads[:, : 2 * span], gate_kept, dims, preferred_element_type=jnp.float32
        ) + lax.dot_general(
            grads[:, 2 * span :], up_kept, dims, preferred_element_type=jnp.float32
        )
        out[...] = total.reshape(groups, rows, tile).astype(out.dtype)

    whole = pl.BlockSpec((2, rows, span), lambda j, *_: (0, 0, 0))
    weight_spec = pl.BlockSpec(
        (tile, gate.shape[1]), lambda j, place, *_: (side_of(place) * tiles + j, 0)
    )
    return pl.pallas_call(
        kernel,
        grid_spec=pltpu.PrefetchScalarGridSpec(
            num_scalar_prefetch=3,
            grid=(tiles,),
            in_specs=[whole] * len(pieces) + [weight_spec, weight_spec],
            out_specs=pl.BlockSpec((groups, rows, tile), lambda j, *_: (0, 0, j)),
            scratch_shapes=[pltpu.VMEM((groups, rows, 4 * span), jnp.bfloat16)],
        ),
        out_shape=jax.ShapeDtypeStruct(
            (groups, rows, width), jnp.float32 if own_side else jnp.bfloat16
        ),
        compiler_params=pltpu.CompilerParams(vmem_limit_bytes=VMEM_BYTES),
        cost_estimate=pl.CostEstimate(
            flops=2 * groups * rows * 4 * span * width,
            bytes_accessed=8 * span * (groups * rows + width) + 4 * groups * rows * width,
            transcendentals=0,
        ),
    )(place, gate_flags, up_flags, *pieces, gate, up)


def down_product(place, flags, parts, halves):
    groups, rows, width = parts[0][0].shape
    n_parts = len(parts)
    group_rows = n_parts * rows
    span = halves[0][0].shape[1]
    tile = min(512, span)
    steps = span // tile
    blocks = tile // BLOCK

    def kernel(place, flags, *refs):
        first, second = refs[:groups], refs[groups : 2 * groups]
        columns, refs = refs[2 * groups : 2 * groups + 2 * n_parts], refs[2 * groups + 2 * n_parts :]
        out, hidden, grads = refs
        step = pl.program_id(0)

        @pl.when(step == 0)
        def _():
            low = place[0] == 0
            for rel in range(groups):
                for p in range(n_parts):
                    start = rel * group_rows + p * rows
                    fill_columns(grads, start, low, columns[2 * p][rel], columns[2 * p + 1][rel])

        @pl.when(step < steps)
        def _():
            for rel in range(groups):
                hidden[rel * group_rows : (rel + 1) * group_rows, :] = first[rel][...]

        @pl.when(step >= steps)
        def _():
            for rel in range(groups):
                hidden[rel * group_rows : (rel + 1) * group_rows, :] = second[rel][...]

        total = lax.dot_general(
            hidden[...], grads[...], (((0,), (0,)), ((), ())), preferred_element_type=jnp.float32
        )
        out[...] = keep_blocks(total, lambda i, j: flags[step * blocks + i, j]).astype(out.dtype)

    full = pl.BlockSpec((groups, rows, width), lambda j, *_: (0, 0, 0))
    first_spec = pl.BlockSpec((group_rows, tile), lambda j, *_: (0, jnp.minimum(j, steps - 1)))
    second_spec = pl.BlockSpec((group_rows, tile), lambda j, *_: (0, jnp.maximum(j - steps, 0)))
    return pl.pallas_call(
        kernel,
        grid_spec=pltpu.PrefetchScalarGridSpec(
            num_scalar_prefetch=2,
            grid=(2 * steps,),
            in_specs=[first_spec] * groups + [second_spec] * groups + [full] * (2 * n_parts),
            out_specs=pl.BlockSpec((tile, 2 * width), lambda j, *_: (j, 0)),
            scratch_shapes=[
                pltpu.VMEM((groups * group_rows, tile), jnp.bfloat16),
                pltpu.VMEM((groups * group_rows, 2 * width), jnp.bfloat16),
            ],
        ),
        out_shape=jax.ShapeDtypeStruct((2 * span, 2 * width), jnp.bfloat16),
        compiler_params=pltpu.CompilerParams(vmem_limit_bytes=VMEM_BYTES),
        cost_estimate=pl.CostEstimate(
            flops=8 * groups * group_rows * span * width,
            bytes_accessed=4 * groups * group_rows * (span + width) + 8 * span * width,
            transcendentals=0,
        ),
    )(place, flags, *halves[0], *halves[1], *[x for part in parts for x in part])


def after(x, *others):
    return lax.optimization_barrier((x, others))[0]


def per_device(
    tokens, out_grad, gate_weight, up_weight, down_weight, gate_mask, up_mask, down_mask
):
    n_f = lax.axis_size("fsdp")
    n_t = lax.axis_size("tensor")
    assert n_t == 2 * n_f and n_f & (n_f - 1) == 0
    bits = n_f.bit_length() - 1
    rows, width = tokens.shape
    sub = rows // n_f
    f_index = lax.axis_index("fsdp")
    t_index = lax.axis_index("tensor")
    plane = t_index // 2
    place = jnp.reshape(t_index % 2, (1,)).astype(jnp.int32)
    bit_orders = (tuple(range(bits)), tuple(reversed(range(bits))))

    def group_order(bit_order):
        order = []
        for i in range(n_f):
            order.append(sum(((i >> (bits - 1 - p)) & 1) << b for p, b in enumerate(bit_order)))
        return tuple(order)

    def across(x, k):
        return lax.ppermute(x, "fsdp", [(f, f ^ k) for f in range(n_f)])

    def along(x, k):
        return lax.ppermute(x, "tensor", [(t, t ^ (2 * k)) for t in range(n_t)])

    def exchange(x):
        return lax.ppermute(x, "tensor", [(t, t ^ 1) for t in range(n_t)])

    def reordered(x, index):
        for b in range(bits):
            pairs = x.reshape(-1, 2, 1 << b, *x.shape[1:])
            flipped = pairs[:, ::-1].reshape(x.shape)
            x = jnp.where((index >> b) & 1 == 1, flipped, x)
        return x

    def swapped(x, move):
        return jnp.stack([x[0]] + [move(x[k], k) for k in range(1, n_f)])

    def own_flags(mask, weight, row, col):
        rb, cb = weight.shape[0] // BLOCK, weight.shape[1] // BLOCK
        return lax.dynamic_slice(mask, (row * rb, col * cb), (rb, cb))

    gate_flags = own_flags(gate_mask, gate_weight, f_index, t_index)
    up_flags = own_flags(up_mask, up_weight, f_index, t_index)
    down_flags = own_flags(down_mask, down_weight, t_index, f_index)

    both = jnp.stack([tokens.reshape(n_f, sub, width), out_grad.reshape(n_f, sub, width)], axis=1)
    both = swapped(reordered(both, plane), along)
    both = swapped(reordered(both, plane ^ f_index), across)
    x_own, g_own = both[:, 0], both[:, 1]

    def part_of(pieces):
        own = jnp.concatenate(pieces, axis=1)
        return own, exchange(own)

    def owner_sum(kept, sent, bit_order):
        for bit in bit_order:
            total = kept.astype(jnp.float32) + across(sent, 1 << bit).astype(jnp.float32)
            groups, low = total.shape[0], total.astype(jnp.bfloat16)
            kept, sent = low[: groups // 2], low[groups // 2 :]
        return total[0]

    def gathered(piece, bit_order):
        held = {0: piece}
        for bit in bit_order:
            for rel in list(held):
                held[rel | 1 << bit] = across(held[rel], 1 << bit)
        return [held[rel] for rel in range(n_f)]

    def forward(parts, weights, flags, transposed, previous=()):
        products = []
        for half in range(2):
            turn = after(place, *previous)
            order = group_order(bit_orders[half])
            products.append(forward_half(turn, weights, flags, parts, order, half, transposed))
            previous = products[-1]
        return products

    def sums(products):
        return [owner_sum(*products[half], bit_orders[half]) for half in range(2)]

    projections = ([gate_weight, up_weight], [gate_flags, up_flags], False)
    near = [x_own] + [along(x_own, k) for k in range(1, n_f // 2)]
    far_own = after(x_own, near[-1])
    far = [along(far_own, k) for k in range(n_f // 2, n_f)]
    part_a = part_of(near)
    products_a = forward([part_a], *projections)
    part_b = part_of(far)
    products_b = forward([part_b], *projections, products_a[1])
    g_start = after(g_own, far[-1], products_a[1])
    g_parts = [part_of([g_start] + [along(g_start, k) for k in range(1, n_f)])]
    products_g = forward(g_parts, [down_weight], [down_flags], True)
    pre = [sums(products_a), sums(products_b)]
    hidden_grad = sums(products_g)

    part_rows = rows // 2
    grads, hidden = [[], []], [[], []]
    for half in range(2):
        for p in range(2):
            v, u = pre[p][half][0], pre[p][half][1]
            d = hidden_grad[half][0, p * part_rows : (p + 1) * part_rows]
            sig = jax.nn.sigmoid(v)
            act = v * sig
            hidden[half].append((act * u).astype(jnp.bfloat16))
            gate_grad = d * u * (sig * (1.0 + v * (1.0 - sig)))
            grads[p].append(jnp.stack([gate_grad, d * act]).astype(jnp.bfloat16))

    def chip_sum(pieces, *previous):
        args = (gate_flags, up_flags, pieces, gate_weight, up_weight, width)
        for_core = input_side(after(place, *previous), *args, False)
        mine = input_side(after(place, for_core), *args, True)
        return mine + exchange(for_core).astype(jnp.float32), mine

    def both_halves(p):
        return [x for half in range(2) for x in gathered(grads[p][half], bit_orders[half])]

    hidden_pieces = [
        gathered(jnp.concatenate(hidden[half]), bit_orders[half]) for half in range(2)
    ]
    far_part, far_mine = chip_sum(
        both_halves(1), *[x for held in hidden_pieces for x in held[:-1]]
    )
    near_part, near_mine = chip_sum(both_halves(0), far_mine)
    def to_rows(part):
        part = part.astype(jnp.bfloat16)
        terms = [part[0]] + [across(part[m], m) for m in range(1, n_f)]
        for b in range(bits):
            odd = ((plane ^ f_index) >> b) & 1 == 1
            terms = [jnp.where(odd, terms[i ^ (1 << b)], x) for i, x in enumerate(terms)]
        return terms

    terms = [jnp.concatenate(x) for x in zip(to_rows(near_part), to_rows(far_part))]
    total = jnp.zeros((n_f, sub, width), jnp.float32)
    for k in range(n_f):
        term = along(terms[k], k) if k else terms[k]
        axes = [bits - 1 - b for b in range(bits) if (k >> b) & 1]
        flipped = jnp.flip(term.reshape((2,) * bits + (sub, width)), axes)
        total = total + flipped.reshape(n_f, sub, width).astype(jnp.float32)
    input_grad = reordered(total.astype(jnp.bfloat16), plane).reshape(rows, width)
    down_grad = down_product(after(place, *terms), down_flags, g_parts, hidden_pieces)
    return (input_grad, down_grad)


def solution(mesh):
    return jax.shard_map(
        per_device,
        mesh=mesh,
        in_specs=(
            P("fsdp", "tensor"),
            P("fsdp", "tensor"),
            P("fsdp", "tensor"),
            P("fsdp", "tensor"),
            P("tensor", "fsdp"),
            P(),
            P(),
            P(),
        ),
        out_specs=(P("fsdp", "tensor"), P("tensor", "fsdp")),
        check_vma=False,
    )
```
